32 devices in a mesh: space: 16 (over z, x, core), scen: 2 (over y).
Axes of the slice: x: 2, y: 2, z: 4, core: 2. Of those that a mesh axis runs over, the one named last changes fastest.
Arguments:
- concentration: float32 [2, 8, 6, 384, 384], P('scen', None, None, 'space'), may hold values from -6 to 6
- emissions: float32 [2, 6, 384, 384], P('scen', None, 'space'), may hold values from -3 to 3
- courant: float32 [2, 8, 6, 384, 384], P(None, None, None, 'space'), may hold values from -0.9 to 0.9
- tile_source: int32 [8640], P('space'), may hold values from 0 to 431, as said below
- tile_target: int32 [8640], P('space'), may hold values from 0 to 511, as said below
- intersection: bfloat16 [8640, 128, 128], P('space'), may hold values from 0 to 0.0625
Outputs:
- transported: float32 [2, 8, 6, 384, 384], P('scen', None, None, 'space')
- regridded: float32 [2, 8, 512, 128], P('scen', None, 'space')
- ensemble_moments: float32 [2, 8, 512, 128], P(None, None, 'space')
The draws below stay inside these ranges and needn't reach their ends.
Inputs may be any that keep to these rules, and one draw needn't show every extreme that they name: `tile_source`: every source block of a row band is named by at least one of the band's tiles. `tile_target`: latitude band b holds target blocks b * 32 to (b+1) * 32 - 1. The 540 tiles of one row band name at most 67 blocks of any one latitude band and at least 31 of every latitude band but one, which receives exactly 67 tiles from every row band. Every target block is named by some tile.
All inputs are finite; a program needn't handle non-finite values.
Results may differ from the reference program's by a relative error of at most 0.0027.
Values sent between devices are 32-bit elements; how exact they have to be, the bound alone decides.
A program may use at most 128 MiB of HBM per device.

```python
import jax
import jax.numpy as jnp
from jax import lax

LEV = 8
C = 384
BLK = 128
TGT_DEV = 32
R = 24
BANDS = 16
SCEN = 2
TILES_DEV = 540
CAP = 67
BASE = 31
TGT_BLKS = 512


def draw_tile_source(key, part):
    blocks = 6 * R * C // BLK

    def one_band(band_key):
        first_key, second_key, third_key = jax.random.split(band_key, 3)
        covered = jax.random.permutation(first_key, blocks).astype(jnp.int32)
        extra_blocks = jax.random.randint(second_key, (TILES_DEV - blocks,), 0, blocks).astype(jnp.int32)
        return jax.random.permutation(third_key, jnp.concatenate([covered, extra_blocks]))
    band_keys = jax.random.split(jax.random.fold_in(key, 3), BANDS)
    return jax.vmap(one_band)(band_keys).reshape(-1).astype(jnp.int32)


def draw_tile_target(key, part):
    hot_key, band_key, order_key = jax.random.split(jax.random.fold_in(key, 5), 3)
    hottest = jax.random.randint(hot_key, (), 0, BANDS).astype(jnp.int32)
    others = jnp.arange(BANDS - 1, dtype=jnp.int32)
    others = others + (others >= hottest).astype(jnp.int32)
    spare_count = TILES_DEV - CAP - (BANDS - 1) * BASE

    def one_band(single_key):
        pick_key, mix_key = jax.random.split(single_key)
        candidates = jnp.repeat(others, CAP - BASE)
        chosen = jax.random.permutation(pick_key, candidates)[:spare_count]
        owners = jnp.concatenate([jnp.full((CAP,), hottest, jnp.int32), jnp.repeat(others, BASE), chosen.astype(jnp.int32)])
        return jax.random.permutation(mix_key, owners)
    owners = jax.vmap(one_band)(jax.random.split(band_key, BANDS)).reshape(-1).astype(jnp.int32)
    marked = (owners[:, None] == jnp.arange(BANDS, dtype=jnp.int32)[None, :]).astype(jnp.int32)
    ranking = jnp.sum((jnp.cumsum(marked, axis=0) - marked) * marked, axis=1).astype(jnp.int32)

    def one_table(single_key):
        return jax.random.permutation(single_key, TGT_DEV).astype(jnp.int32)
    tables = jax.vmap(one_table)(jax.random.split(order_key, BANDS))
    blocks = tables[owners, ranking % TGT_DEV]
    return (owners * TGT_DEV + blocks).astype(jnp.int32)


def shard_levels(key, dims, shards, smallest, largest):
    def one(dim, blocks):
        draws = jax.random.uniform(jax.random.fold_in(jax.random.fold_in(key, 6), dim), (blocks,), jnp.float32, smallest / len(shards), largest / len(shards))
        return jnp.repeat(jnp.exp(draws), dims[dim] // blocks).reshape((-1,) + (1,) * (len(dims) - dim - 1))

    loudness = one(*shards[0])
    for cut in shards[1:]:
        loudness = loudness * one(*cut)
    return loudness


def scatter_about(stream_key, dims, spread, reach, shards=(), kind=jnp.bfloat16):
    values = spread * jax.random.normal(stream_key, dims, jnp.float32)
    if shards:
        values = values * shard_levels(stream_key, dims, shards, -0.22, 0.18)
    return jnp.clip(values, -reach, reach).astype(kind)


def setup_inputs(seed: int = 0) -> dict:
    key_list = jax.random.split(jax.random.key(seed), 7)
    concentration = scatter_about(key_list[0], (SCEN, LEV, 6, C, C), 1.0, 6.0, ((0, 2), (3, 16)), jnp.float32)
    emissions = scatter_about(key_list[1], (SCEN, 6, C, C), 0.5, 3.0, ((0, 2), (2, 16)), jnp.float32)
    courant = jnp.clip(jax.random.uniform(key_list[2], (2, LEV, 6, C, C), jnp.float32, -0.9, 0.9) * shard_levels(key_list[2], (2, LEV, 6, C, C), ((3, 16),), -0.4, 0.0), -0.9, 0.9)
    tile_source = draw_tile_source(jax.random.fold_in(key_list[6], 71), 0)
    tile_target = draw_tile_target(jax.random.fold_in(key_list[6], 71), 0)
    intersection = jnp.clip(0.0625 * jax.random.uniform(key_list[5], (TILES_DEV * BANDS, BLK, BLK), jnp.float32) ** shard_levels(key_list[5], (TILES_DEV * BANDS, BLK, BLK), ((0, 16),), -0.2, 0.2), 0.0, 0.0625).astype(jnp.bfloat16)
    return dict(concentration=concentration, emissions=emissions, courant=courant, tile_source=tile_source, tile_target=tile_target, intersection=intersection)


def parabola_sweep(padded, courant_faces, sweep_axis):
    cells_along = padded.shape[sweep_axis] - 6

    def window(values_in, first_cell, length):
        return lax.slice_in_dim(values_in, first_cell, first_cell + length, axis=sweep_axis)

    edge_values = (7.0 / 12.0) * (window(padded, 1, cells_along + 3) + window(padded, 2, cells_along + 3)) - (1.0 / 12.0) * (window(padded, 0, cells_along + 3) + window(padded, 3, cells_along + 3))
    left_edge = window(edge_values, 0, cells_along + 2)
    right_edge = window(edge_values, 1, cells_along + 2)
    centre = window(padded, 2, cells_along + 2)
    slopes = right_edge - left_edge
    curvature = 6.0 * centre - 3.0 * (left_edge + right_edge)
    backward = -courant_faces
    upwind_left = courant_faces * (window(right_edge, 0, cells_along + 1) - 0.5 * courant_faces * (window(slopes, 0, cells_along + 1) - (1.0 - 2.0 * courant_faces / 3.0) * window(curvature, 0, cells_along + 1)))
    upwind_right = courant_faces * (window(left_edge, 1, cells_along + 1) + 0.5 * backward * (window(slopes, 1, cells_along + 1) + (1.0 - 2.0 * backward / 3.0) * window(curvature, 1, cells_along + 1)))
    fluxes = jnp.where(courant_faces >= 0.0, upwind_left, upwind_right)
    return window(padded, 3, cells_along) - (window(fluxes, 1, cells_along) - window(fluxes, 0, cells_along))


def column_pad(tracer, east_wind, north_wind):
    padded_faces = []
    speed_faces = []
    for face_number in range(6):
        if face_number % 2 == 0:
            source = tracer[:, (face_number - 2) % 6, C - 3:, :]
            west_cells = jnp.swapaxes(jnp.flip(source, -1), -1, -2)
            west_speed = jnp.flip(north_wind[:, (face_number - 2) % 6, C - 1, :], -1)
            east_cells = tracer[:, (face_number + 1) % 6, :, 0:3]
            east_speed = east_wind[:, (face_number + 1) % 6, :, 0]
        else:
            west_cells = tracer[:, (face_number - 1) % 6, :, C - 3:]
            west_speed = east_wind[:, (face_number - 1) % 6, :, C - 1]
            source = tracer[:, (face_number + 2) % 6, 0:3, :]
            east_cells = jnp.swapaxes(jnp.flip(source, -1), -1, -2)
            east_speed = jnp.flip(north_wind[:, (face_number + 2) % 6, 0, :], -1)
        padded_faces.append(jnp.concatenate([west_cells, tracer[:, face_number], east_cells], -1))
        speeds = jnp.concatenate([west_speed[:, :, None], east_wind[:, face_number], east_speed[:, :, None]], -1)
        speed_faces.append(0.5 * (speeds[:, :, :-1] + speeds[:, :, 1:]))
    return jnp.stack(padded_faces, 1), jnp.stack(speed_faces, 1)


def row_pad(tracer, east_wind, north_wind):
    padded_faces = []
    speed_faces = []
    for face_number in range(6):
        if face_number % 2 == 0:
            north_cells = jnp.swapaxes(jnp.flip(tracer[:, (face_number + 2) % 6, :, 0:3], -2), -1, -2)
            north_speed = jnp.flip(east_wind[:, (face_number + 2) % 6, :, 0], -1)
            south_cells = tracer[:, (face_number - 1) % 6, C - 3:, :]
            south_speed = north_wind[:, (face_number - 1) % 6, C - 1, :]
        else:
            north_cells = tracer[:, (face_number + 1) % 6, 0:3, :]
            north_speed = north_wind[:, (face_number + 1) % 6, 0, :]
            south_cells = jnp.swapaxes(jnp.flip(tracer[:, (face_number - 2) % 6, :, C - 3:], -2), -1, -2)
            south_speed = jnp.flip(east_wind[:, (face_number - 2) % 6, :, C - 1], -1)
        padded_faces.append(jnp.concatenate([south_cells, tracer[:, face_number], north_cells], -2))
        speeds = jnp.concatenate([south_speed[:, None, :], north_wind[:, face_number], north_speed[:, None, :]], -2)
        speed_faces.append(0.5 * (speeds[:, :-1, :] + speeds[:, 1:, :]))
    return jnp.stack(padded_faces, 1), jnp.stack(speed_faces, 1)


def reference(concentration, emissions, courant, tile_source, tile_target, intersection):
    east_wind = courant[0]
    north_wind = courant[1]

    def advance(scenario_pair):
        tracer = scenario_pair[0].at[0].add(scenario_pair[1])
        for step_number in range(2):
            padded, courant_faces = column_pad(tracer, east_wind, north_wind)
            tracer = parabola_sweep(padded, courant_faces, 3)
            padded, courant_faces = row_pad(tracer, east_wind, north_wind)
            tracer = parabola_sweep(padded, courant_faces, 2)
        return tracer

    transported = lax.map(advance, (concentration, emissions))

    def add_band(band_number, accumulated):
        start_row = (band_number * R).astype(jnp.int32)
        start_tile = (band_number * TILES_DEV).astype(jnp.int32)
        rows_taken = lax.dynamic_slice_in_dim(transported, start_row, R, axis=3)
        rounded = lax.optimization_barrier(rows_taken.astype(jnp.bfloat16)).astype(jnp.float32)
        blocks = rounded.reshape(SCEN * LEV, -1, BLK)
        sources = lax.dynamic_slice_in_dim(tile_source, start_tile, TILES_DEV).astype(jnp.int32)
        targets = lax.dynamic_slice_in_dim(tile_target, start_tile, TILES_DEV).astype(jnp.int32)
        weights = lax.dynamic_slice_in_dim(intersection, start_tile, TILES_DEV, axis=0).astype(jnp.float32)
        chosen = jnp.take(blocks, sources, axis=1)
        partial_value = jnp.einsum("btk,tkc->btc", chosen, weights, precision=lax.Precision.HIGHEST)
        return accumulated.at[:, targets].add(partial_value)

    accumulated = lax.fori_loop(0, BANDS, add_band, jnp.zeros((SCEN * LEV, TGT_BLKS, BLK), jnp.float32))
    regridded = accumulated.reshape(SCEN, LEV, TGT_BLKS, BLK)
    moments = jnp.stack([jnp.sum(regridded, 0), jnp.sum(regridded * regridded, 0)]) / SCEN
    return transported, regridded, moments
```

```python
import functools

import jax
import jax.numpy as jnp
from jax import lax
from jax.experimental import pallas as pl
from jax.experimental.pallas import tpu as pltpu
from jax.sharding import PartitionSpec as P

TGT_DEV = 32


def broadcast(value, axis, source):
    kept = jnp.where(lax.axis_index(axis) == source, value, 0).astype(value.dtype)
    return lax.psum(kept, axis)


def from_behind(block, axis, distance):
    devices = range(lax.axis_size(axis))
    route = [((i - distance) % len(devices), i) for i in devices]
    return lax.ppermute(block, axis, route)


def parabola_sweep(padded, courant_faces, sweep_axis):
    cells_along = padded.shape[sweep_axis] - 6

    def window(values_in, first_cell, length):
        return lax.slice_in_dim(values_in, first_cell, first_cell + length, axis=sweep_axis)

    edge_values = 7.0 / 12.0 * (
        window(padded, 1, cells_along + 3) + window(padded, 2, cells_along + 3)
    ) - 1.0 / 12.0 * (window(padded, 0, cells_along + 3) + window(padded, 3, cells_along + 3))
    left_edge = window(edge_values, 0, cells_along + 2)
    right_edge = window(edge_values, 1, cells_along + 2)
    centre = window(padded, 2, cells_along + 2)
    slopes = right_edge - left_edge
    curvature = 6.0 * centre - 3.0 * (left_edge + right_edge)
    backward = -courant_faces
    upwind_left = courant_faces * (
        window(right_edge, 0, cells_along + 1)
        - 0.5
        * courant_faces
        * (
            window(slopes, 0, cells_along + 1)
            - (1.0 - 2.0 * courant_faces / 3.0) * window(curvature, 0, cells_along + 1)
        )
    )
    upwind_right = courant_faces * (
        window(left_edge, 1, cells_along + 1)
        + 0.5
        * backward
        * (
            window(slopes, 1, cells_along + 1)
            + (1.0 - 2.0 * backward / 3.0) * window(curvature, 1, cells_along + 1)
        )
    )
    fluxes = jnp.where(courant_faces >= 0.0, upwind_left, upwind_right)
    return window(padded, 3, cells_along) - (
        window(fluxes, 1, cells_along) - window(fluxes, 0, cells_along)
    )


def pack_rows(tracer, north_wind, lowest):
    row_count = tracer.shape[3]
    width_cells = tracer.shape[4]
    if lowest:
        layers = tracer[:, :, :, 0:3, :]
        wind_row = north_wind[:, :, 0:1, :]
    else:
        layers = tracer[:, :, :, row_count - 3 :, :]
        wind_row = north_wind[:, :, row_count - 1 :, :]
    return jnp.concatenate([layers.reshape(-1, width_cells), wind_row.reshape(-1, width_cells)], 0)


def unpack_rows(packed, tracer_shape):
    split_at = tracer_shape[0] * tracer_shape[1] * 18
    layers = packed[:split_at].reshape(tracer_shape[0], tracer_shape[1], 6, 3, packed.shape[1])
    wind_row = packed[split_at:].reshape(tracer_shape[1], 6, packed.shape[1])
    return (layers, wind_row)


def column_halos(tracer, east_wind, north_wind, position, band_count):
    row_count = tracer.shape[3]
    width_cells = tracer.shape[4]
    received = []
    for root_rank, lowest in ((band_count - 1, False), (0, True)):
        packed = pack_rows(tracer, north_wind, lowest)
        received.append(unpack_rows(broadcast(packed, "space", root_rank), tracer.shape))
    top_layers, top_wind = received[0]
    low_layers, low_wind = received[1]
    start_column = width_cells - (position + 1) * row_count
    padded_faces = []
    speed_faces = []
    for face_number in range(6):
        if face_number % 2 == 0:
            source = lax.dynamic_slice_in_dim(
                top_layers[:, :, (face_number - 2) % 6], start_column, row_count, axis=3
            )
            west_cells = jnp.swapaxes(jnp.flip(source, -1), -1, -2)
            west_speed = jnp.flip(
                lax.dynamic_slice_in_dim(
                    top_wind[:, (face_number - 2) % 6], start_column, row_count, axis=1
                ),
                -1,
            )
            east_cells = tracer[:, :, (face_number + 1) % 6, :, 0:3]
            east_speed = east_wind[:, (face_number + 1) % 6, :, 0]
        else:
            west_cells = tracer[:, :, (face_number - 1) % 6, :, width_cells - 3 :]
            west_speed = east_wind[:, (face_number - 1) % 6, :, width_cells - 1]
            source = lax.dynamic_slice_in_dim(
                low_layers[:, :, (face_number + 2) % 6], start_column, row_count, axis=3
            )
            east_cells = jnp.swapaxes(jnp.flip(source, -1), -1, -2)
            east_speed = jnp.flip(
                lax.dynamic_slice_in_dim(
                    low_wind[:, (face_number + 2) % 6], start_column, row_count, axis=1
                ),
                -1,
            )
        padded_faces.append(
            jnp.concatenate([west_cells, tracer[:, :, face_number], east_cells], -1)
        )
        speeds = jnp.concatenate(
            [west_speed[:, :, None], east_wind[:, face_number], east_speed[:, :, None]], -1
        )
        speed_faces.append(0.5 * (speeds[:, :, :-1] + speeds[:, :, 1:]))
    return (jnp.stack(padded_faces, 2), jnp.stack(speed_faces, 1))


def row_halos(tracer, east_wind, north_wind, position, band_count):
    scenarios = tracer.shape[0]
    levels = tracer.shape[1]
    row_count = tracer.shape[3]
    width_cells = tracer.shape[4]
    shifted = []
    for step_by, lowest in ((-1, True), (1, False)):
        packed = pack_rows(tracer, north_wind, lowest)
        shifted.append(unpack_rows(from_behind(packed, "space", step_by), tracer.shape))
    above_layers, above_wind = shifted[0]
    below_layers, below_wind = shifted[1]
    columns = jnp.concatenate([tracer[..., 0:3], tracer[..., width_cells - 3 :]], -1)
    columns = jnp.swapaxes(columns, -1, -2).reshape(-1, row_count)
    column_speed = jnp.stack([east_wind[..., 0], east_wind[..., width_cells - 1]], -2).reshape(
        -1, row_count
    )
    gathered = lax.all_gather(
        jnp.concatenate([columns, column_speed], 0), "space", axis=1, tiled=True
    )
    split_at = scenarios * levels * 36
    edge_layers = gathered[:split_at].reshape(scenarios, levels, 6, 6, -1)
    edge_speed = gathered[split_at:].reshape(levels, 6, 2, -1)
    at_top = position == band_count - 1
    at_bottom = position == 0
    padded_faces = []
    speed_faces = []
    for face_number in range(6):
        if face_number % 2 == 0:
            north_cells = jnp.where(
                at_top,
                jnp.flip(edge_layers[:, :, (face_number + 2) % 6, 0:3], -1),
                above_layers[:, :, face_number],
            )
            north_speed = jnp.where(
                at_top,
                jnp.flip(edge_speed[:, (face_number + 2) % 6, 0], -1),
                above_wind[:, face_number],
            )
            south_cells = jnp.where(
                at_bottom,
                below_layers[:, :, (face_number - 1) % 6],
                below_layers[:, :, face_number],
            )
            south_speed = jnp.where(
                at_bottom, below_wind[:, (face_number - 1) % 6], below_wind[:, face_number]
            )
        else:
            north_cells = jnp.where(
                at_top, above_layers[:, :, (face_number + 1) % 6], above_layers[:, :, face_number]
            )
            north_speed = jnp.where(
                at_top, above_wind[:, (face_number + 1) % 6], above_wind[:, face_number]
            )
            south_cells = jnp.where(
                at_bottom,
                jnp.flip(edge_layers[:, :, (face_number - 2) % 6, 3:6], -1),
                below_layers[:, :, face_number],
            )
            south_speed = jnp.where(
                at_bottom,
                jnp.flip(edge_speed[:, (face_number - 2) % 6, 1], -1),
                below_wind[:, face_number],
            )
        padded_faces.append(
            jnp.concatenate([south_cells, tracer[:, :, face_number], north_cells], -2)
        )
        speeds = jnp.concatenate(
            [south_speed[:, None, :], north_wind[:, face_number], north_speed[:, None, :]], -2
        )
        speed_faces.append(0.5 * (speeds[:, :-1, :] + speeds[:, 1:, :]))
    return (jnp.stack(padded_faces, 2), jnp.stack(speed_faces, 1))


def largest_divisor(number, limit):
    return max(d for d in range(1, limit + 1) if number % d == 0)


def regrid_kernel(rows, chunk, group, source_ref, target_ref, block_ref, weight_ref, sum_ref):
    step = pl.program_id(0)

    @pl.when(step == 0)
    def _():
        sum_ref[...] = jnp.zeros_like(sum_ref)

    def body(index, carry):
        products = []
        for member in range(group):
            local_tile = index * group + member
            source = source_ref[step * chunk + local_tile]
            cells = block_ref[pl.ds(pl.multiple_of(source * rows, rows), rows), :]
            products.append(
                jnp.dot(
                    cells.astype(jnp.bfloat16),
                    weight_ref[local_tile],
                    preferred_element_type=jnp.float32,
                )
            )
        for member in range(group):
            target = target_ref[step * chunk + index * group + member]
            place = pl.ds(pl.multiple_of(target * rows, rows), rows)
            sum_ref[place, :] = sum_ref[place, :] + products[member]
        return carry

    lax.fori_loop(0, chunk // group, body, 0)


def regrid(tile_source, tile_target, blocks, intersection, rows, targets):
    tiles, cells = intersection.shape[0], intersection.shape[1]
    chunk = largest_divisor(tiles, 60)
    group = largest_divisor(chunk, 20)
    summed = pl.pallas_call(
        functools.partial(regrid_kernel, rows, chunk, group),
        grid=(tiles // chunk,),
        out_shape=jax.ShapeDtypeStruct((targets * rows, cells), jnp.float32),
        in_specs=[
            pl.BlockSpec(memory_space=pltpu.SMEM),
            pl.BlockSpec(memory_space=pltpu.SMEM),
            pl.BlockSpec(memory_space=pltpu.VMEM),
            pl.BlockSpec((chunk, cells, cells), lambda step: (step, 0, 0)),
        ],
        out_specs=pl.BlockSpec(memory_space=pltpu.VMEM),
        compiler_params=pltpu.CompilerParams(vmem_limit_bytes=40 * 1024 * 1024),
        cost_estimate=pl.CostEstimate(
            flops=2 * tiles * rows * cells * cells,
            bytes_accessed=2 * tiles * cells * cells,
            transcendentals=0,
        ),
    )(tile_source, tile_target, blocks, intersection)
    return summed.reshape(targets, rows, cells)


def local(concentration, emissions, courant, tile_source, tile_target, intersection):
    band_count = lax.axis_size("space")
    position = lax.axis_index("space")
    tracer = concentration.at[:, 0].add(emissions)
    east_wind = courant[0]
    north_wind = courant[1]
    for step_number in range(2):
        padded, courant_faces = column_halos(tracer, east_wind, north_wind, position, band_count)
        tracer = parabola_sweep(padded, courant_faces, 4)
        padded, courant_faces = row_halos(tracer, east_wind, north_wind, position, band_count)
        tracer = parabola_sweep(padded, courant_faces, 3)
    scenarios = tracer.shape[0]
    levels = tracer.shape[1]
    batch_rows = scenarios * levels
    block_cells = intersection.shape[1]
    blocks = tracer.reshape(batch_rows, -1, block_cells)
    blocks = jnp.swapaxes(blocks, 0, 1).reshape(-1, block_cells)
    band_sums = regrid(
        tile_source, tile_target, blocks, intersection, batch_rows, TGT_DEV * band_count
    )
    summed = lax.psum_scatter(
        band_sums,
        "space",
        scatter_dimension=0,
        tiled=True,
    )
    band_result = jnp.swapaxes(summed, 0, 1)
    regridded = band_result.reshape(scenarios, levels, TGT_DEV, block_cells)
    moment_sums = jnp.stack([jnp.sum(regridded, 0), jnp.sum(regridded * regridded, 0)])
    summed_moments = lax.psum(moment_sums, "scen")
    ensemble_moments = summed_moments / (scenarios * lax.axis_size("scen"))
    return (tracer, regridded, ensemble_moments)


def solution(mesh):
    return jax.shard_map(
        local,
        mesh=mesh,
        in_specs=(
            P("scen", None, None, "space", None),
            P("scen", None, "space", None),
            P(None, None, None, "space", None),
            P("space"),
            P("space"),
            P("space", None, None),
        ),
        out_specs=(
            P("scen", None, None, "space", None),
            P("scen", None, "space", None),
            P(None, None, "space", None),
        ),
        check_vma=False,
    )
```

```python
import functools

import jax
import jax.numpy as jnp
from jax import lax
from jax.experimental import pallas as pl
from jax.experimental.pallas import tpu as pltpu
from jax.sharding import PartitionSpec as P

TGT_DEV = 32


MESH = pl.DeviceIdType.MESH
HIGHEST = lax.Precision.HIGHEST


def parabola_sweep(values, courant_faces, axis):
    count = values.shape[axis]
    behind = pltpu.roll(values, 1, axis)
    edges = (7.0 / 12.0) * (behind + values) - (1.0 / 12.0) * (
        pltpu.roll(values, 2, axis) + pltpu.roll(values, count - 1, axis)
    )
    forward = courant_faces >= 0.0
    speed = jnp.abs(courant_faces)
    far = jnp.where(forward, pltpu.roll(edges, 1, axis), pltpu.roll(edges, count - 1, axis))
    centre = jnp.where(forward, behind, values)
    curvature = 6.0 * centre - 3.0 * (edges + far)
    flux = courant_faces * (
        edges + 0.5 * speed * ((far - edges) + (1.0 - (2.0 / 3.0) * speed) * curvature)
    )
    return values - (pltpu.roll(flux, count - 1, axis) - flux)


def transport_kernel(
    bands,
    conc_ref,
    emis_ref,
    wind_ref,
    out_ref,
    block_ref,
    tracer,
    east,
    north,
    edge_pack,
    edge_turned,
    top_edge,
    low_edge,
    even_columns,
    odd_columns,
    gathered,
    turned,
    rows_up,
    rows_down,
    from_south,
    from_north,
    edge_send,
    edge_recv,
    column_send,
    column_recv,
    row_send,
    row_recv,
):
    me = lax.axis_index("space")
    top = bands - 1
    levels, rows, width = conc_ref.shape[1], conc_ref.shape[3], conc_ref.shape[4]
    tall, full = tracer.shape[2], tracer.shape[3]
    held = edge_turned.shape[2]
    slots = edge_pack.shape[1]
    at_top, at_low = me == top, me == 0

    barrier = pltpu.get_barrier_semaphore()

    def greet(band, carry):
        @pl.when(band != me)
        def _():
            pl.semaphore_signal(barrier, inc=1, device_id={"space": band}, device_id_type=MESH)

        return carry

    lax.fori_loop(0, bands, greet, 0)

    across = lax.broadcasted_iota(jnp.int32, (width, width), 0) + lax.broadcasted_iota(
        jnp.int32, (width, width), 1
    )
    mirror = (across == width - 1).astype(jnp.float32)
    lane = lax.broadcasted_iota(jnp.int32, (held, 128), 1)

    def load(level, carry):
        extra = jnp.where(level == 0, 1.0, 0.0)
        for face in range(6):
            tracer[level, face, 0:rows, 0:width] = (
                conc_ref[0, level, face] + extra * emis_ref[0, face]
            )
        return carry

    lax.fori_loop(0, levels, load, 0)
    even_columns[...] = jnp.zeros_like(even_columns)
    odd_columns[...] = jnp.zeros_like(odd_columns)
    edge_pack[...] = jnp.zeros_like(edge_pack)
    edge_turned[...] = jnp.zeros_like(edge_turned)

    def edge_copy(step, band, target):
        is_top = target is top_edge
        return pltpu.make_async_remote_copy(
            src_ref=edge_turned.at[step, band],
            dst_ref=target.at[step],
            send_sem=edge_send.at[step, band],
            recv_sem=edge_recv.at[step, 0 if is_top else 1],
            device_id={"space": band},
            device_id_type=MESH,
        )

    def column_copy(step, source, band, to_top):
        return pltpu.make_async_remote_copy(
            src_ref=source.at[step],
            dst_ref=gathered.at[step, band],
            send_sem=column_send.at[step, 0 if to_top else 1],
            recv_sem=column_recv.at[step, band],
            device_id={"space": top if to_top else 0},
            device_id_type=MESH,
        )

    def row_copies(step):
        upward = pltpu.make_async_remote_copy(
            src_ref=rows_up.at[step],
            dst_ref=from_south.at[step],
            send_sem=row_send.at[step, 0],
            recv_sem=row_recv.at[step, 0],
            device_id={"space": lax.rem(me + 1, bands)},
            device_id_type=MESH,
        )
        downward = pltpu.make_async_remote_copy(
            src_ref=rows_down.at[step],
            dst_ref=from_north.at[step],
            send_sem=row_send.at[step, 1],
            recv_sem=row_recv.at[step, 1],
            device_id={"space": lax.rem(me + bands - 1, bands)},
            device_id_type=MESH,
        )
        return upward, downward

    def each_other(action):
        def body(band, carry):
            @pl.when(band != me)
            def _():
                action(band)

            return carry

        lax.fori_loop(0, bands, body, 0)

    for step in range(2):
        for is_top, own, target in ((True, at_top, top_edge), (False, at_low, low_edge)):

            @pl.when(own)
            def _(step=step, is_top=is_top, target=target):
                def pack(level, carry):
                    for pair in range(3):
                        face = 2 * pair if is_top else 2 * pair + 1
                        first = rows - 3 if is_top else 0
                        edge_pack[level, 3 * pair : 3 * pair + 3, :] = tracer[
                            level, face, first : first + 3, 0:width
                        ]
                        if step == 0:
                            row = rows - 1 if is_top else 0
                            edge_pack[level, 9 + pair : 10 + pair, :] = wind_ref[
                                1, level, face, row : row + 1, :
                            ]
                    return carry

                lax.fori_loop(0, levels, pack, 0)
                flat = edge_pack[...].reshape(levels * slots, width)
                result = lax.dot_general(
                    mirror,
                    flat,
                    (((1,), (1,)), ((), ())),
                    precision=HIGHEST,
                    preferred_element_type=jnp.float32,
                )
                for band in range(bands):
                    edge_turned[step, band, 0:rows, :] = result[band * rows : (band + 1) * rows]

        if step == 0:
            pl.semaphore_wait(barrier, bands - 1)
        for own, target in ((at_top, top_edge), (at_low, low_edge)):

            @pl.when(own)
            def _(step=step, target=target):
                each_other(lambda band: edge_copy(step, band, target).start())
                target[step] = edge_turned[step, me]

            @pl.when(jnp.logical_not(own))
            def _(step=step, target=target):
                edge_copy(step, me, target).wait_recv()

        def sweep_east(level, carry, step=step):
            top_part = top_edge[step]
            low_part = low_edge[step]

            def moved(part, place, lane_to):
                shift = lax.rem(lane_to - place + 256, 128)
                return pltpu.roll(part, shift, 1)

            halves = lane[0:rows] >= 64
            for face in range(6):
                if face % 2 == 0:
                    base = level * slots + 3 * (((face - 2) % 6) // 2)
                    west_cells = moved(top_part, base, 125)[0:rows]
                    east_cells = tracer[level, (face + 1) % 6, 0:rows, 0:128]
                else:
                    west_cells = tracer[level, face - 1, 0:rows, width - 128 : width]
                    base = level * slots + 3 * (((face + 2) % 6) // 2)
                    east_cells = moved(low_part, base, 0)[0:rows]
                tracer[level, face, 0:rows, width:full] = jnp.where(
                    halves, west_cells, east_cells
                )
                if step == 0:
                    if face % 2 == 0:
                        base = level * slots + 9 + ((face - 2) % 6) // 2
                        west_wind = moved(top_part, base, 127)[0:rows]
                        east_wind = wind_ref[0, level, (face + 1) % 6, :, 0:128]
                    else:
                        west_wind = wind_ref[0, level, face - 1, :, width - 128 : width]
                        base = level * slots + 9 + ((face + 2) % 6) // 2
                        east_wind = moved(low_part, base, 0)[0:rows]
                    east[level, face, 0:rows, 0:width] = wind_ref[0, level, face]
                    east[level, face, 0:rows, width:full] = jnp.where(
                        halves, west_wind, east_wind
                    )
                    cells = east[level, face]
                    east[level, face] = 0.5 * (pltpu.roll(cells, 1, 1) + cells)
            for face in range(6):
                swept = parabola_sweep(tracer[level, face, 0:held, :], east[level, face], 1)
                tracer[level, face, 0:rows, 0:width] = swept[0:rows, 0:width]
                rows_down[step, level, 3 * face : 3 * face + 3, :] = swept[0:3, 0:width]
                rows_up[step, level, 3 * face : 3 * face + 3, :] = swept[rows - 3 : rows, 0:width]
                base = level * slots + 3 * (face // 2)
                if face % 2 == 0:
                    edge = jnp.where(lane < 3, swept[:, 0:128], 0.0)
                    even_columns[step] = even_columns[step] + moved(edge, 0, base)
                else:
                    edge = jnp.where(lane >= 125, swept[:, width - 128 : width], 0.0)
                    odd_columns[step] = odd_columns[step] + moved(edge, 125, base)
                if step == 0:
                    rows_down[step, level, 18 + face : 19 + face, :] = wind_ref[1, level, face, 0:1, :]
                    rows_up[step, level, 18 + face : 19 + face, :] = wind_ref[
                        1, level, face, rows - 1 : rows, :
                    ]
                    base = level * slots + 9 + face // 2
                    some = lane[0:rows]
                    if face % 2 == 0:
                        edge = jnp.where(some < 1, wind_ref[0, level, face, :, 0:128], 0.0)
                        even_columns[step, 0:rows] = even_columns[step, 0:rows] + moved(
                            edge, 0, base
                        )
                    else:
                        edge = jnp.where(
                            some >= 127, wind_ref[0, level, face, :, width - 128 : width], 0.0
                        )
                        odd_columns[step, 0:rows] = odd_columns[step, 0:rows] + moved(
                            edge, 127, base
                        )
            return carry

        lax.fori_loop(0, levels, sweep_east, 0)

        upward, downward = row_copies(step)
        upward.start()
        downward.start()
        for own, source, to_top in ((at_top, even_columns, True), (at_low, odd_columns, False)):

            @pl.when(jnp.logical_not(own))
            def _(step=step, source=source, to_top=to_top):
                column_copy(step, source, me, to_top).start()

            @pl.when(own)
            def _(step=step, source=source, to_top=to_top):
                gathered[step, me] = source[step]
                each_other(lambda band: column_copy(step, source, band, to_top).wait_recv())
                strips = [gathered[step, band, 0:rows, :] for band in range(bands)]
                columns = jnp.concatenate(strips, 0)
                result = jnp.dot(
                    jnp.transpose(columns),
                    mirror,
                    precision=HIGHEST,
                    preferred_element_type=jnp.float32,
                )
                turned[...] = result.reshape(levels, slots, width)

        upward.wait_recv()
        downward.wait_recv()

        def sweep_north(level, carry, step=step):
            for face in range(6):
                north_face, south_face = face, face
                if face % 2 == 0:
                    pair = ((face + 2) % 6) // 2
                    beyond = from_north[step, level, 3 * face : 3 * face + 3, :]
                    beyond = jnp.where(at_top, turned[level, 3 * pair : 3 * pair + 3, :], beyond)
                    other = (face - 1) % 6
                    before = jnp.where(
                        at_low,
                        from_south[step, level, 3 * other : 3 * other + 3, :],
                        from_south[step, level, 3 * face : 3 * face + 3, :],
                    )
                else:
                    other = (face + 1) % 6
                    beyond = jnp.where(
                        at_top,
                        from_north[step, level, 3 * other : 3 * other + 3, :],
                        from_north[step, level, 3 * face : 3 * face + 3, :],
                    )
                    pair = ((face - 2) % 6) // 2
                    before = from_south[step, level, 3 * face : 3 * face + 3, :]
                    before = jnp.where(at_low, turned[level, 3 * pair : 3 * pair + 3, :], before)
                tracer[level, face, rows : rows + 3, 0:width] = beyond
                tracer[level, face, tall - 3 : tall, 0:width] = before
                if step == 0:
                    own_row = 18 + face
                    other_row = 18 + other
                    turned_wind = turned[level, 9 + pair : 10 + pair, :]
                    beyond = from_north[step, level, own_row : own_row + 1, :]
                    before = from_south[step, level, own_row : own_row + 1, :]
                    if face % 2 == 0:
                        beyond = jnp.where(at_top, turned_wind, beyond)
                        before = jnp.where(
                            at_low, from_south[step, level, other_row : other_row + 1, :], before
                        )
                    else:
                        beyond = jnp.where(
                            at_top, from_north[step, level, other_row : other_row + 1, :], beyond
                        )
                        before = jnp.where(at_low, turned_wind, before)
                    north[level, face, 0:rows, :] = wind_ref[1, level, face]
                    north[level, face, rows : rows + 1, :] = beyond
                    north[level, face, tall - 1 : tall, :] = before
                    cells = north[level, face]
                    north[level, face] = 0.5 * (pltpu.roll(cells, 1, 0) + cells)
                swept = parabola_sweep(tracer[level, face, :, 0:width], north[level, face], 0)
                if step == 0:
                    tracer[level, face, 0:rows, 0:width] = swept[0:rows]
                else:
                    out_ref[0, level, face] = swept[0:rows]
                    parts = width // 128
                    for part in range(parts):
                        start = face * rows * parts * levels + part * levels + level
                        block_ref[pl.ds(start, rows, stride=parts * levels), :] = swept[
                            0:rows, part * 128 : (part + 1) * 128
                        ]
            return carry

        lax.fori_loop(0, levels, sweep_north, 0)

    for step in range(2):
        for own, target in ((at_top, top_edge), (at_low, low_edge)):

            @pl.when(own)
            def _(step=step, target=target):
                each_other(lambda band: edge_copy(step, band, target).wait_send())

        for own, source, to_top in ((at_top, even_columns, True), (at_low, odd_columns, False)):

            @pl.when(jnp.logical_not(own))
            def _(step=step, source=source, to_top=to_top):
                column_copy(step, source, me, to_top).wait_send()

        upward, downward = row_copies(step)
        upward.wait_send()
        downward.wait_send()


def transport(concentration, emissions, courant):
    bands = lax.axis_size("space")
    _, levels, faces, rows, width = concentration.shape
    held = -(-rows // 8) * 8
    tall = -(-(rows + 6) // 8) * 8
    full = width + 128
    slots = 128 // levels
    f32 = jnp.float32
    vmem = pl.BlockSpec(memory_space=pltpu.VMEM)
    return pl.pallas_call(
        functools.partial(transport_kernel, bands),
        out_shape=(
            jax.ShapeDtypeStruct(concentration.shape, f32),
            jax.ShapeDtypeStruct((faces * rows * (width // 128) * levels, 128), f32),
        ),
        in_specs=[vmem] * 3,
        out_specs=(vmem, vmem),
        scratch_shapes=[
            pltpu.VMEM((levels, faces, tall, full), f32),
            pltpu.VMEM((levels, faces, held, full), f32),
            pltpu.VMEM((levels, faces, tall, width), f32),
            pltpu.VMEM((levels, slots, width), f32),
            pltpu.VMEM((2, bands, held, 128), f32),
            pltpu.VMEM((2, held, 128), f32),
            pltpu.VMEM((2, held, 128), f32),
            pltpu.VMEM((2, held, 128), f32),
            pltpu.VMEM((2, held, 128), f32),
            pltpu.VMEM((2, bands, held, 128), f32),
            pltpu.VMEM((levels, slots, width), f32),
            pltpu.VMEM((2, levels, 24, width), f32),
            pltpu.VMEM((2, levels, 24, width), f32),
            pltpu.VMEM((2, levels, 24, width), f32),
            pltpu.VMEM((2, levels, 24, width), f32),
            pltpu.SemaphoreType.DMA((2, bands)),
            pltpu.SemaphoreType.DMA((2, 2)),
            pltpu.SemaphoreType.DMA((2, 2)),
            pltpu.SemaphoreType.DMA((2, bands)),
            pltpu.SemaphoreType.DMA((2, 2)),
            pltpu.SemaphoreType.DMA((2, 2)),
        ],
        compiler_params=pltpu.CompilerParams(
            collective_id=0, has_side_effects=True, vmem_limit_bytes=52 * 1024 * 1024
        ),
    )(concentration, emissions, courant)


def largest_divisor(number, limit):
    return max(d for d in range(1, limit + 1) if number % d == 0)


def regrid_kernel(rows, chunk, group, source_ref, target_ref, block_ref, weight_ref, sum_ref):
    step = pl.program_id(0)

    @pl.when(step == 0)
    def _():
        sum_ref[...] = jnp.zeros_like(sum_ref)

    def body(index, carry):
        products = []
        for member in range(group):
            local_tile = index * group + member
            source = source_ref[step * chunk + local_tile]
            cells = block_ref[pl.ds(pl.multiple_of(source * rows, rows), rows), :]
            products.append(
                jnp.dot(
                    cells.astype(jnp.bfloat16),
                    weight_ref[local_tile],
                    preferred_element_type=jnp.float32,
                )
            )
        for member in range(group):
            target = target_ref[step * chunk + index * group + member]
            place = pl.ds(pl.multiple_of(target * rows, rows), rows)
            sum_ref[place, :] = sum_ref[place, :] + products[member]
        return carry

    lax.fori_loop(0, chunk // group, body, 0)


def regrid(tile_source, tile_target, blocks, intersection, rows, targets):
    tiles, cells = intersection.shape[0], intersection.shape[1]
    chunk = largest_divisor(tiles, 60)
    group = largest_divisor(chunk, 20)
    summed = pl.pallas_call(
        functools.partial(regrid_kernel, rows, chunk, group),
        grid=(tiles // chunk,),
        out_shape=jax.ShapeDtypeStruct((targets * rows, cells), jnp.float32),
        in_specs=[
            pl.BlockSpec(memory_space=pltpu.SMEM),
            pl.BlockSpec(memory_space=pltpu.SMEM),
            pl.BlockSpec(memory_space=pltpu.VMEM),
            pl.BlockSpec((chunk, cells, cells), lambda step: (step, 0, 0)),
        ],
        out_specs=pl.BlockSpec(memory_space=pltpu.VMEM),
        compiler_params=pltpu.CompilerParams(vmem_limit_bytes=40 * 1024 * 1024),
        cost_estimate=pl.CostEstimate(
            flops=2 * tiles * rows * cells * cells,
            bytes_accessed=2 * tiles * cells * cells,
            transcendentals=0,
        ),
    )(tile_source, tile_target, blocks, intersection)
    return summed.reshape(targets, rows, cells)


def local(concentration, emissions, courant, tile_source, tile_target, intersection):
    band_count = lax.axis_size("space")
    tracer, blocks = transport(concentration, emissions, courant)
    scenarios = tracer.shape[0]
    levels = tracer.shape[1]
    batch_rows = scenarios * levels
    block_cells = intersection.shape[1]
    band_sums = regrid(
        tile_source, tile_target, blocks, intersection, batch_rows, TGT_DEV * band_count
    )
    summed = lax.psum_scatter(
        band_sums,
        "space",
        scatter_dimension=0,
        tiled=True,
    )
    band_result = jnp.swapaxes(summed, 0, 1)
    regridded = band_result.reshape(scenarios, levels, TGT_DEV, block_cells)
    moment_sums = jnp.stack([jnp.sum(regridded, 0), jnp.sum(regridded * regridded, 0)])
    summed_moments = lax.psum(moment_sums, "scen")
    ensemble_moments = summed_moments / (scenarios * lax.axis_size("scen"))
    return (tracer, regridded, ensemble_moments)


def solution(mesh):
    return jax.shard_map(
        local,
        mesh=mesh,
        in_specs=(
            P("scen", None, None, "space", None),
            P("scen", None, "space", None),
            P(None, None, None, "space", None),
            P("space"),
            P("space"),
            P("space", None, None),
        ),
        out_specs=(
            P("scen", None, None, "space", None),
            P("scen", None, "space", None),
            P(None, None, "space", None),
        ),
        check_vma=False,
    )
```

```python
import functools

import jax
import jax.numpy as jnp
from jax import lax
from jax.experimental import pallas as pl
from jax.experimental.pallas import tpu as pltpu
from jax.sharding import PartitionSpec as P

TGT_DEV = 32


MESH = pl.DeviceIdType.MESH
HIGHEST = lax.Precision.HIGHEST


def parabola_sweep(values, courant_faces, axis):
    count = values.shape[axis]
    behind = pltpu.roll(values, 1, axis)
    edges = (7.0 / 12.0) * (behind + values) - (1.0 / 12.0) * (
        pltpu.roll(values, 2, axis) + pltpu.roll(values, count - 1, axis)
    )
    forward = courant_faces >= 0.0
    speed = jnp.abs(courant_faces)
    far = jnp.where(forward, pltpu.roll(edges, 1, axis), pltpu.roll(edges, count - 1, axis))
    centre = jnp.where(forward, behind, values)
    curvature = 6.0 * centre - 3.0 * (edges + far)
    flux = courant_faces * (
        edges + 0.5 * speed * ((far - edges) + (1.0 - (2.0 / 3.0) * speed) * curvature)
    )
    return values - (pltpu.roll(flux, count - 1, axis) - flux)


def transport_kernel(
    bands,
    conc_ref,
    emis_ref,
    wind_ref,
    out_ref,
    block_ref,
    tracer,
    east,
    north,
    edge_pack,
    edge_turned,
    top_edge,
    low_edge,
    even_columns,
    odd_columns,
    gathered,
    turned,
    rows_up,
    rows_down,
    from_south,
    from_north,
    edge_send,
    edge_recv,
    column_send,
    column_recv,
    row_send,
    row_recv,
):
    me = lax.axis_index("space")
    top = bands - 1
    levels, rows, width = conc_ref.shape[1], conc_ref.shape[3], conc_ref.shape[4]
    tall, full = tracer.shape[2], tracer.shape[3]
    held = edge_turned.shape[2]
    slots = edge_pack.shape[1]
    at_top, at_low = me == top, me == 0

    barrier = pltpu.get_barrier_semaphore()

    def greet(band, carry):
        @pl.when(band != me)
        def _():
            pl.semaphore_signal(barrier, inc=1, device_id={"space": band}, device_id_type=MESH)

        return carry

    lax.fori_loop(0, bands, greet, 0)

    across = lax.broadcasted_iota(jnp.int32, (width, width), 0) + lax.broadcasted_iota(
        jnp.int32, (width, width), 1
    )
    mirror = (across == width - 1).astype(jnp.float32)
    lane = lax.broadcasted_iota(jnp.int32, (held, 128), 1)

    def load(level, carry):
        extra = jnp.where(level == 0, 1.0, 0.0)
        for face in range(6):
            tracer[level, face, 0:rows, 0:width] = (
                conc_ref[0, level, face] + extra * emis_ref[0, face]
            )
        return carry

    lax.fori_loop(0, levels, load, 0)
    even_columns[...] = jnp.zeros_like(even_columns)
    odd_columns[...] = jnp.zeros_like(odd_columns)
    edge_pack[...] = jnp.zeros_like(edge_pack)
    edge_turned[...] = jnp.zeros_like(edge_turned)

    def edge_copy(step, band, target):
        is_top = target is top_edge
        return pltpu.make_async_remote_copy(
            src_ref=edge_turned.at[step, band],
            dst_ref=target.at[step],
            send_sem=edge_send.at[step, band],
            recv_sem=edge_recv.at[step, 0 if is_top else 1],
            device_id={"space": band},
            device_id_type=MESH,
        )

    def column_copy(step, source, band, to_top):
        return pltpu.make_async_remote_copy(
            src_ref=source.at[step],
            dst_ref=gathered.at[step, band],
            send_sem=column_send.at[step, 0 if to_top else 1],
            recv_sem=column_recv.at[step, band],
            device_id={"space": top if to_top else 0},
            device_id_type=MESH,
        )

    def row_copies(step):
        upward = pltpu.make_async_remote_copy(
            src_ref=rows_up.at[step],
            dst_ref=from_south.at[step],
            send_sem=row_send.at[step, 0],
            recv_sem=row_recv.at[step, 0],
            device_id={"space": lax.rem(me + 1, bands)},
            device_id_type=MESH,
        )
        downward = pltpu.make_async_remote_copy(
            src_ref=rows_down.at[step],
            dst_ref=from_north.at[step],
            send_sem=row_send.at[step, 1],
            recv_sem=row_recv.at[step, 1],
            device_id={"space": lax.rem(me + bands - 1, bands)},
            device_id_type=MESH,
        )
        return upward, downward

    def each_other(action):
        def body(band, carry):
            @pl.when(band != me)
            def _():
                action(band)

            return carry

        lax.fori_loop(0, bands, body, 0)

    for step in range(2):
        for is_top, own, target in ((True, at_top, top_edge), (False, at_low, low_edge)):

            @pl.when(own)
            def _(step=step, is_top=is_top, target=target):
                def pack(level, carry):
                    for pair in range(3):
                        face = 2 * pair if is_top else 2 * pair + 1
                        first = rows - 3 if is_top else 0
                        edge_pack[level, 3 * pair : 3 * pair + 3, :] = tracer[
                            level, face, first : first + 3, 0:width
                        ]
                        if step == 0:
                            row = rows - 1 if is_top else 0
                            edge_pack[level, 9 + pair : 10 + pair, :] = wind_ref[
                                1, level, face, row : row + 1, :
                            ]
                    return carry

                lax.fori_loop(0, levels, pack, 0)
                flat = edge_pack[...].reshape(levels * slots, width)
                result = lax.dot_general(
                    mirror,
                    flat,
                    (((1,), (1,)), ((), ())),
                    precision=HIGHEST,
                    preferred_element_type=jnp.float32,
                )
                for band in range(bands):
                    edge_turned[step, band, 0:rows, :] = result[band * rows : (band + 1) * rows]

        if step == 0:
            pl.semaphore_wait(barrier, bands - 1)
        for own, target in ((at_top, top_edge), (at_low, low_edge)):

            @pl.when(own)
            def _(step=step, target=target):
                each_other(lambda band: edge_copy(step, band, target).start())
                target[step] = edge_turned[step, me]

            @pl.when(jnp.logical_not(own))
            def _(step=step, target=target):
                edge_copy(step, me, target).wait_recv()

        def sweep_east(level, carry, step=step):
            top_part = top_edge[step]
            low_part = low_edge[step]

            def moved(part, place, lane_to):
                shift = lax.rem(lane_to - place + 256, 128)
                return pltpu.roll(part, shift, 1)

            halves = lane[0:rows] >= 64
            for face in range(6):
                if face % 2 == 0:
                    base = level * slots + 3 * (((face - 2) % 6) // 2)
                    west_cells = moved(top_part, base, 125)[0:rows]
                    east_cells = tracer[level, (face + 1) % 6, 0:rows, 0:128]
                else:
                    west_cells = tracer[level, face - 1, 0:rows, width - 128 : width]
                    base = level * slots + 3 * (((face + 2) % 6) // 2)
                    east_cells = moved(low_part, base, 0)[0:rows]
                tracer[level, face, 0:rows, width:full] = jnp.where(
                    halves, west_cells, east_cells
                )
                if step == 0:
                    if face % 2 == 0:
                        base = level * slots + 9 + ((face - 2) % 6) // 2
                        west_wind = moved(top_part, base, 127)[0:rows]
                        east_wind = wind_ref[0, level, (face + 1) % 6, :, 0:128]
                    else:
                        west_wind = wind_ref[0, level, face - 1, :, width - 128 : width]
                        base = level * slots + 9 + ((face + 2) % 6) // 2
                        east_wind = moved(low_part, base, 0)[0:rows]
                    east[level, face, 0:rows, 0:width] = wind_ref[0, level, face]
                    east[level, face, 0:rows, width:full] = jnp.where(
                        halves, west_wind, east_wind
                    )
                    cells = east[level, face]
                    east[level, face] = 0.5 * (pltpu.roll(cells, 1, 1) + cells)
            for face in range(6):
                swept = parabola_sweep(tracer[level, face, 0:held, :], east[level, face], 1)
                tracer[level, face, 0:rows, 0:width] = swept[0:rows, 0:width]
                rows_down[step, level, 3 * face : 3 * face + 3, :] = swept[0:3, 0:width]
                rows_up[step, level, 3 * face : 3 * face + 3, :] = swept[rows - 3 : rows, 0:width]
                base = level * slots + 3 * (face // 2)
                if face % 2 == 0:
                    edge = jnp.where(lane < 3, swept[:, 0:128], 0.0)
                    even_columns[step] = even_columns[step] + moved(edge, 0, base)
                else:
                    edge = jnp.where(lane >= 125, swept[:, width - 128 : width], 0.0)
                    odd_columns[step] = odd_columns[step] + moved(edge, 125, base)
                if step == 0:
                    rows_down[step, level, 18 + face : 19 + face, :] = wind_ref[1, level, face, 0:1, :]
                    rows_up[step, level, 18 + face : 19 + face, :] = wind_ref[
                        1, level, face, rows - 1 : rows, :
                    ]
                    base = level * slots + 9 + face // 2
                    some = lane[0:rows]
                    if face % 2 == 0:
                        edge = jnp.where(some < 1, wind_ref[0, level, face, :, 0:128], 0.0)
                        even_columns[step, 0:rows] = even_columns[step, 0:rows] + moved(
                            edge, 0, base
                        )
                    else:
                        edge = jnp.where(
                            some >= 127, wind_ref[0, level, face, :, width - 128 : width], 0.0
                        )
                        odd_columns[step, 0:rows] = odd_columns[step, 0:rows] + moved(
                            edge, 127, base
                        )
            return carry

        lax.fori_loop(0, levels, sweep_east, 0)

        upward, downward = row_copies(step)
        upward.start()
        downward.start()
        for own, source, to_top in ((at_top, even_columns, True), (at_low, odd_columns, False)):

            @pl.when(jnp.logical_not(own))
            def _(step=step, source=source, to_top=to_top):
                column_copy(step, source, me, to_top).start()

            @pl.when(own)
            def _(step=step, source=source, to_top=to_top):
                gathered[step, me] = source[step]
                each_other(lambda band: column_copy(step, source, band, to_top).wait_recv())
                strips = [gathered[step, band, 0:rows, :] for band in range(bands)]
                columns = jnp.concatenate(strips, 0)
                result = jnp.dot(
                    jnp.transpose(columns),
                    mirror,
                    precision=HIGHEST,
                    preferred_element_type=jnp.float32,
                )
                turned[...] = result.reshape(levels, slots, width)

        upward.wait_recv()
        downward.wait_recv()

        def sweep_north(level, carry, step=step):
            for face in range(6):
                north_face, south_face = face, face
                if face % 2 == 0:
                    pair = ((face + 2) % 6) // 2
                    beyond = from_north[step, level, 3 * face : 3 * face + 3, :]
                    beyond = jnp.where(at_top, turned[level, 3 * pair : 3 * pair + 3, :], beyond)
                    other = (face - 1) % 6
                    before = jnp.where(
                        at_low,
                        from_south[step, level, 3 * other : 3 * other + 3, :],
                        from_south[step, level, 3 * face : 3 * face + 3, :],
                    )
                else:
                    other = (face + 1) % 6
                    beyond = jnp.where(
                        at_top,
                        from_north[step, level, 3 * other : 3 * other + 3, :],
                        from_north[step, level, 3 * face : 3 * face + 3, :],
                    )
                    pair = ((face - 2) % 6) // 2
                    before = from_south[step, level, 3 * face : 3 * face + 3, :]
                    before = jnp.where(at_low, turned[level, 3 * pair : 3 * pair + 3, :], before)
                tracer[level, face, rows : rows + 3, 0:width] = beyond
                tracer[level, face, tall - 3 : tall, 0:width] = before
                if step == 0:
                    own_row = 18 + face
                    other_row = 18 + other
                    turned_wind = turned[level, 9 + pair : 10 + pair, :]
                    beyond = from_north[step, level, own_row : own_row + 1, :]
                    before = from_south[step, level, own_row : own_row + 1, :]
                    if face % 2 == 0:
                        beyond = jnp.where(at_top, turned_wind, beyond)
                        before = jnp.where(
                            at_low, from_south[step, level, other_row : other_row + 1, :], before
                        )
                    else:
                        beyond = jnp.where(
                            at_top, from_north[step, level, other_row : other_row + 1, :], beyond
                        )
                        before = jnp.where(at_low, turned_wind, before)
                    north[level, face, 0:rows, :] = wind_ref[1, level, face]
                    north[level, face, rows : rows + 1, :] = beyond
                    north[level, face, tall - 1 : tall, :] = before
                    cells = north[level, face]
                    north[level, face] = 0.5 * (pltpu.roll(cells, 1, 0) + cells)
                swept = parabola_sweep(tracer[level, face, :, 0:width], north[level, face], 0)
                if step == 0:
                    tracer[level, face, 0:rows, 0:width] = swept[0:rows]
                else:
                    out_ref[0, level, face] = swept[0:rows]
                    parts = width // 128
                    for part in range(parts):
                        start = face * rows * parts * levels + part * levels + level
                        block_ref[pl.ds(start, rows, stride=parts * levels), :] = swept[
                            0:rows, part * 128 : (part + 1) * 128
                        ]
            return carry

        lax.fori_loop(0, levels, sweep_north, 0)

    for step in range(2):
        for own, target in ((at_top, top_edge), (at_low, low_edge)):

            @pl.when(own)
            def _(step=step, target=target):
                each_other(lambda band: edge_copy(step, band, target).wait_send())

        for own, source, to_top in ((at_top, even_columns, True), (at_low, odd_columns, False)):

            @pl.when(jnp.logical_not(own))
            def _(step=step, source=source, to_top=to_top):
                column_copy(step, source, me, to_top).wait_send()

        upward, downward = row_copies(step)
        upward.wait_send()
        downward.wait_send()


def transport(concentration, emissions, courant):
    bands = lax.axis_size("space")
    _, levels, faces, rows, width = concentration.shape
    held = -(-rows // 8) * 8
    tall = -(-(rows + 6) // 8) * 8
    full = width + 128
    slots = 128 // levels
    f32 = jnp.float32
    vmem = pl.BlockSpec(memory_space=pltpu.VMEM)
    return pl.pallas_call(
        functools.partial(transport_kernel, bands),
        out_shape=(
            jax.ShapeDtypeStruct(concentration.shape, f32),
            jax.ShapeDtypeStruct((faces * rows * (width // 128) * levels, 128), f32),
        ),
        in_specs=[vmem] * 3,
        out_specs=(vmem, vmem),
        scratch_shapes=[
            pltpu.VMEM((levels, faces, tall, full), f32),
            pltpu.VMEM((levels, faces, held, full), f32),
            pltpu.VMEM((levels, faces, tall, width), f32),
            pltpu.VMEM((levels, slots, width), f32),
            pltpu.VMEM((2, bands, held, 128), f32),
            pltpu.VMEM((2, held, 128), f32),
            pltpu.VMEM((2, held, 128), f32),
            pltpu.VMEM((2, held, 128), f32),
            pltpu.VMEM((2, held, 128), f32),
            pltpu.VMEM((2, bands, held, 128), f32),
            pltpu.VMEM((levels, slots, width), f32),
            pltpu.VMEM((2, levels, 24, width), f32),
            pltpu.VMEM((2, levels, 24, width), f32),
            pltpu.VMEM((2, levels, 24, width), f32),
            pltpu.VMEM((2, levels, 24, width), f32),
            pltpu.SemaphoreType.DMA((2, bands)),
            pltpu.SemaphoreType.DMA((2, 2)),
            pltpu.SemaphoreType.DMA((2, 2)),
            pltpu.SemaphoreType.DMA((2, bands)),
            pltpu.SemaphoreType.DMA((2, 2)),
            pltpu.SemaphoreType.DMA((2, 2)),
        ],
        compiler_params=pltpu.CompilerParams(
            collective_id=0, has_side_effects=True, vmem_limit_bytes=52 * 1024 * 1024
        ),
    )(concentration, emissions, courant)


def largest_divisor(number, limit):
    return max(d for d in range(1, limit + 1) if number % d == 0)


def regrid_kernel(rows, chunk, group, source_ref, target_ref, block_ref, weight_ref, sum_ref):
    step = pl.program_id(0)

    @pl.when(step == 0)
    def _():
        sum_ref[...] = jnp.zeros_like(sum_ref)

    def body(index, carry):
        products = []
        for member in range(group):
            local_tile = index * group + member
            source = source_ref[step * chunk + local_tile]
            cells = block_ref[pl.ds(pl.multiple_of(source * rows, rows), rows), :]
            products.append(
                jnp.dot(
                    cells.astype(jnp.bfloat16),
                    weight_ref[local_tile],
                    preferred_element_type=jnp.float32,
                )
            )
        for member in range(group):
            target = target_ref[step * chunk + index * group + member]
            place = pl.ds(pl.multiple_of(target * rows, rows), rows)
            sum_ref[place, :] = sum_ref[place, :] + products[member]
        return carry

    lax.fori_loop(0, chunk // group, body, 0)


def regrid(tile_source, tile_target, blocks, intersection, rows, targets):
    tiles, cells = intersection.shape[0], intersection.shape[1]
    chunk = largest_divisor(tiles, 60)
    group = largest_divisor(chunk, 20)
    summed = pl.pallas_call(
        functools.partial(regrid_kernel, rows, chunk, group),
        grid=(tiles // chunk,),
        out_shape=jax.ShapeDtypeStruct((targets * rows, cells), jnp.float32),
        in_specs=[
            pl.BlockSpec(memory_space=pltpu.SMEM),
            pl.BlockSpec(memory_space=pltpu.SMEM),
            pl.BlockSpec(memory_space=pltpu.VMEM),
            pl.BlockSpec((chunk, cells, cells), lambda step: (step, 0, 0)),
        ],
        out_specs=pl.BlockSpec(memory_space=pltpu.VMEM),
        compiler_params=pltpu.CompilerParams(vmem_limit_bytes=40 * 1024 * 1024),
        cost_estimate=pl.CostEstimate(
            flops=2 * tiles * rows * cells * cells,
            bytes_accessed=2 * tiles * cells * cells,
            transcendentals=0,
        ),
    )(tile_source, tile_target, blocks, intersection)
    return summed.reshape(targets, rows, cells)


def combine_kernel(
    scenarios,
    part_ref,
    regrid_ref,
    moment_ref,
    core_in,
    pair_sum,
    side_in,
    side_sum,
    far_in,
    mine,
    ensemble,
    core_send,
    core_recv,
    side_send,
    side_recv,
    far_send,
    far_recv,
    scen_send,
    scen_recv,
):
    me = lax.axis_index("space")
    scen = lax.axis_index("scen")
    layers = part_ref.shape[0]
    levels, blocks = regrid_ref.shape[0], regrid_ref.shape[1]
    core, side, layer = lax.rem(me, 2), lax.rem(me // 2, 2), me // 4
    sibling = {"space": me + 1 - 2 * core}
    beside = {"space": me + 2 - 4 * side}

    def far_device(other):
        return {"space": other * 4 + side * 2 + core}

    def ahead(step):
        return lax.rem(layer + step, layers)

    def other_scen(step):
        return lax.rem(scen + step, scenarios)

    barrier = pltpu.get_barrier_semaphore()
    peers = [sibling, beside]
    peers += [far_device(ahead(step)) for step in range(1, layers)]
    peers += [{"scen": other_scen(step)} for step in range(1, scenarios)]
    for peer in peers:
        pl.semaphore_signal(barrier, inc=1, device_id=peer, device_id_type=MESH)
    pl.semaphore_wait(barrier, len(peers))

    def remote(source, target, send_sem, recv_sem, device):
        return pltpu.make_async_remote_copy(
            src_ref=source,
            dst_ref=target,
            send_sem=send_sem,
            recv_sem=recv_sem,
            device_id=device,
            device_id_type=MESH,
        )

    def core_copy(at):
        return remote(
            part_ref.at[at, :, 1 - core], core_in.at[at], core_send.at[at], core_recv.at[at], sibling
        )

    def side_copy(at):
        return remote(
            pair_sum.at[at, 1 - side], side_in.at[at], side_send.at[at], side_recv.at[at], beside
        )

    def far_copy(at):
        return remote(
            side_sum.at[at], far_in.at[layer], far_send.at[at], far_recv.at[layer], far_device(at)
        )

    def far_arrival(at):
        return remote(
            side_sum.at[at], far_in.at[at], far_send.at[at], far_recv.at[at], far_device(at)
        )

    def scen_copy(to, slot):
        return remote(mine, ensemble.at[slot], scen_send.at[to], scen_recv.at[slot], {"scen": to})

    order = [ahead(step) for step in range(1, layers + 1)]
    for at in order:
        core_copy(at).start()
    for at in order:
        core_copy(at).wait_recv()
        pair_sum[at, 1 - side] = part_ref[at, 1 - side, core] + core_in[at, 1 - side]
        side_copy(at).start()
        pair_sum[at, side] = part_ref[at, side, core] + core_in[at, side]
    for at in order:
        side_copy(at).wait_recv()
        side_sum[at] = pair_sum[at, side] + side_in[at]
        if at is not order[-1]:
            far_copy(at).start()
    mine[...] = side_sum[layer]
    for at in order[:-1]:
        far_arrival(at).wait_recv()
        mine[...] = mine[...] + far_in[at]
    for step in range(1, scenarios):
        scen_copy(other_scen(step), scen).start()
    ensemble[scen] = mine[...]
    for level in range(levels):
        regrid_ref[level] = mine[pl.ds(level, blocks, stride=levels), :]
    for step in range(1, scenarios):
        scen_copy(other_scen(step), other_scen(step)).wait_recv()
    mean = ensemble[0]
    square = mean * mean
    for index in range(1, scenarios):
        member = ensemble[index]
        mean = mean + member
        square = square + member * member
    far_in[0] = mean / scenarios
    side_in[0] = square / scenarios
    for level in range(levels):
        moment_ref[0, level] = far_in[0, pl.ds(level, blocks, stride=levels), :]
        moment_ref[1, level] = side_in[0, pl.ds(level, blocks, stride=levels), :]
    for at in order:
        core_copy(at).wait_send()
        side_copy(at).wait_send()
        if at is not order[-1]:
            far_copy(at).wait_send()
    for step in range(1, scenarios):
        scen_copy(other_scen(step), scen).wait_send()


def combine(band_sums, levels):
    bands, scenarios = lax.axis_size("space"), lax.axis_size("scen")
    cells = band_sums.shape[-1]
    layers = bands // 4
    held = TGT_DEV * levels
    f32 = jnp.float32
    vmem = pl.BlockSpec(memory_space=pltpu.VMEM)
    parts = band_sums.reshape(layers, 2, 2, held, cells)
    return pl.pallas_call(
        functools.partial(combine_kernel, scenarios),
        out_shape=(
            jax.ShapeDtypeStruct((levels, TGT_DEV, cells), f32),
            jax.ShapeDtypeStruct((2, levels, TGT_DEV, cells), f32),
        ),
        in_specs=[vmem],
        out_specs=(vmem, vmem),
        scratch_shapes=[
            pltpu.VMEM((layers, 2, held, cells), f32),
            pltpu.VMEM((layers, 2, held, cells), f32),
            pltpu.VMEM((layers, held, cells), f32),
            pltpu.VMEM((layers, held, cells), f32),
            pltpu.VMEM((layers, held, cells), f32),
            pltpu.VMEM((held, cells), f32),
            pltpu.VMEM((scenarios, held, cells), f32),
        ]
        + [pltpu.SemaphoreType.DMA((layers,))] * 6
        + [pltpu.SemaphoreType.DMA((scenarios,))] * 2,
        compiler_params=pltpu.CompilerParams(
            collective_id=1, has_side_effects=True, vmem_limit_bytes=48 * 1024 * 1024
        ),
    )(parts)


def local(concentration, emissions, courant, tile_source, tile_target, intersection):
    band_count = lax.axis_size("space")
    tracer, blocks = transport(concentration, emissions, courant)
    scenarios = tracer.shape[0]
    levels = tracer.shape[1]
    batch_rows = scenarios * levels
    block_cells = intersection.shape[1]
    band_sums = regrid(
        tile_source, tile_target, blocks, intersection, batch_rows, TGT_DEV * band_count
    )
    regridded, ensemble_moments = combine(band_sums, levels)
    return (tracer, regridded[None], ensemble_moments)


def solution(mesh):
    return jax.shard_map(
        local,
        mesh=mesh,
        in_specs=(
            P("scen", None, None, "space", None),
            P("scen", None, "space", None),
            P(None, None, None, "space", None),
            P("space"),
            P("space"),
            P("space", None, None),
        ),
        out_specs=(
            P("scen", None, None, "space", None),
            P("scen", None, "space", None),
            P(None, None, "space", None),
        ),
        check_vma=False,
    )
```

```python
import functools

import jax
import jax.numpy as jnp
from jax import lax
from jax.experimental import pallas as pl
from jax.experimental.pallas import tpu as pltpu
from jax.sharding import PartitionSpec as P

TGT_DEV = 32


MESH = pl.DeviceIdType.MESH
HIGHEST = lax.Precision.HIGHEST


def parabola_sweep(values, courant_faces, axis):
    count = values.shape[axis]
    behind = pltpu.roll(values, 1, axis)
    edges = (7.0 / 12.0) * (behind + values) - (1.0 / 12.0) * (
        pltpu.roll(values, 2, axis) + pltpu.roll(values, count - 1, axis)
    )
    forward = courant_faces >= 0.0
    speed = jnp.abs(courant_faces)
    far = jnp.where(forward, pltpu.roll(edges, 1, axis), pltpu.roll(edges, count - 1, axis))
    centre = jnp.where(forward, behind, values)
    curvature = 6.0 * centre - 3.0 * (edges + far)
    flux = courant_faces * (
        edges + 0.5 * speed * ((far - edges) + (1.0 - (2.0 / 3.0) * speed) * curvature)
    )
    return values - (pltpu.roll(flux, count - 1, axis) - flux)


def transport_kernel(
    bands,
    conc_ref,
    emis_ref,
    wind_ref,
    out_ref,
    block_ref,
    tracer,
    east,
    north,
    edge_pack,
    edge_turned,
    top_edge,
    low_edge,
    even_columns,
    odd_columns,
    gathered,
    turned,
    rows_up,
    rows_down,
    from_south,
    from_north,
    edge_send,
    edge_recv,
    column_send,
    column_recv,
    row_send,
    row_recv,
):
    me = lax.axis_index("space")
    top = bands - 1
    levels, rows, width = conc_ref.shape[1], conc_ref.shape[3], conc_ref.shape[4]
    tall, full = tracer.shape[2], tracer.shape[3]
    held = edge_turned.shape[2]
    slots = edge_pack.shape[1]
    at_top, at_low = me == top, me == 0

    barrier = pltpu.get_barrier_semaphore()

    def greet(band, carry):
        @pl.when(band != me)
        def _():
            pl.semaphore_signal(barrier, inc=1, device_id={"space": band}, device_id_type=MESH)

        return carry

    lax.fori_loop(0, bands, greet, 0)

    across = lax.broadcasted_iota(jnp.int32, (width, width), 0) + lax.broadcasted_iota(
        jnp.int32, (width, width), 1
    )
    mirror = (across == width - 1).astype(jnp.float32)
    lane = lax.broadcasted_iota(jnp.int32, (held, 128), 1)

    def load(level, carry):
        extra = jnp.where(level == 0, 1.0, 0.0)
        for face in range(6):
            tracer[level, face, 0:rows, 0:width] = (
                conc_ref[0, level, face] + extra * emis_ref[0, face]
            )
        return carry

    lax.fori_loop(0, levels, load, 0)
    even_columns[...] = jnp.zeros_like(even_columns)
    odd_columns[...] = jnp.zeros_like(odd_columns)
    edge_pack[...] = jnp.zeros_like(edge_pack)
    edge_turned[...] = jnp.zeros_like(edge_turned)

    def edge_copy(step, band, target):
        is_top = target is top_edge
        return pltpu.make_async_remote_copy(
            src_ref=edge_turned.at[step, band],
            dst_ref=target.at[step],
            send_sem=edge_send.at[step, band],
            recv_sem=edge_recv.at[step, 0 if is_top else 1],
            device_id={"space": band},
            device_id_type=MESH,
        )

    def column_copy(step, source, band, to_top):
        return pltpu.make_async_remote_copy(
            src_ref=source.at[step],
            dst_ref=gathered.at[step, band],
            send_sem=column_send.at[step, 0 if to_top else 1],
            recv_sem=column_recv.at[step, band],
            device_id={"space": top if to_top else 0},
            device_id_type=MESH,
        )

    def row_copies(step, level):
        upward = pltpu.make_async_remote_copy(
            src_ref=rows_up.at[step, level],
            dst_ref=from_south.at[step, level],
            send_sem=row_send.at[step, 0, level],
            recv_sem=row_recv.at[step, 0, level],
            device_id={"space": lax.rem(me + 1, bands)},
            device_id_type=MESH,
        )
        downward = pltpu.make_async_remote_copy(
            src_ref=rows_down.at[step, level],
            dst_ref=from_north.at[step, level],
            send_sem=row_send.at[step, 1, level],
            recv_sem=row_recv.at[step, 1, level],
            device_id={"space": lax.rem(me + bands - 1, bands)},
            device_id_type=MESH,
        )
        return upward, downward

    def each_other(action):
        def body(band, carry):
            @pl.when(band != me)
            def _():
                action(band)

            return carry

        lax.fori_loop(0, bands, body, 0)

    for step in range(2):
        for is_top, own, target in ((True, at_top, top_edge), (False, at_low, low_edge)):

            @pl.when(own)
            def _(step=step, is_top=is_top, target=target):
                def pack(level, carry):
                    for pair in range(3):
                        face = 2 * pair if is_top else 2 * pair + 1
                        first = rows - 3 if is_top else 0
                        edge_pack[level, 3 * pair : 3 * pair + 3, :] = tracer[
                            level, face, first : first + 3, 0:width
                        ]
                        if step == 0:
                            row = rows - 1 if is_top else 0
                            edge_pack[level, 9 + pair : 10 + pair, :] = wind_ref[
                                1, level, face, row : row + 1, :
                            ]
                    return carry

                lax.fori_loop(0, levels, pack, 0)
                flat = edge_pack[...].reshape(levels * slots, width)
                result = lax.dot_general(
                    mirror,
                    flat,
                    (((1,), (1,)), ((), ())),
                    precision=HIGHEST,
                    preferred_element_type=jnp.float32,
                )
                for band in range(bands):
                    edge_turned[step, band, 0:rows, :] = result[band * rows : (band + 1) * rows]

        if step == 0:
            pl.semaphore_wait(barrier, bands - 1)
        for own, target in ((at_top, top_edge), (at_low, low_edge)):

            @pl.when(own)
            def _(step=step, target=target):
                each_other(lambda band: edge_copy(step, band, target).start())
                target[step] = edge_turned[step, me]

            @pl.when(jnp.logical_not(own))
            def _(step=step, target=target):
                edge_copy(step, me, target).wait_recv()

        def sweep_east(level, carry, step=step):
            top_part = top_edge[step]
            low_part = low_edge[step]

            def moved(part, place, lane_to):
                shift = lax.rem(lane_to - place + 256, 128)
                return pltpu.roll(part, shift, 1)

            halves = lane[0:rows] >= 64
            for face in range(6):
                if face % 2 == 0:
                    base = level * slots + 3 * (((face - 2) % 6) // 2)
                    west_cells = moved(top_part, base, 125)[0:rows]
                    east_cells = tracer[level, (face + 1) % 6, 0:rows, 0:128]
                else:
                    west_cells = tracer[level, face - 1, 0:rows, width - 128 : width]
                    base = level * slots + 3 * (((face + 2) % 6) // 2)
                    east_cells = moved(low_part, base, 0)[0:rows]
                tracer[level, face, 0:rows, width:full] = jnp.where(
                    halves, west_cells, east_cells
                )
                if step == 0:
                    if face % 2 == 0:
                        base = level * slots + 9 + ((face - 2) % 6) // 2
                        west_wind = moved(top_part, base, 127)[0:rows]
                        east_wind = wind_ref[0, level, (face + 1) % 6, :, 0:128]
                    else:
                        west_wind = wind_ref[0, level, face - 1, :, width - 128 : width]
                        base = level * slots + 9 + ((face + 2) % 6) // 2
                        east_wind = moved(low_part, base, 0)[0:rows]
                    east[level, face, 0:rows, 0:width] = wind_ref[0, level, face]
                    east[level, face, 0:rows, width:full] = jnp.where(
                        halves, west_wind, east_wind
                    )
                    cells = east[level, face]
                    east[level, face] = 0.5 * (pltpu.roll(cells, 1, 1) + cells)
            for face in range(6):
                swept = parabola_sweep(tracer[level, face, 0:held, :], east[level, face], 1)
                tracer[level, face, 0:rows, 0:width] = swept[0:rows, 0:width]
                rows_down[step, level, 3 * face : 3 * face + 3, :] = swept[0:3, 0:width]
                rows_up[step, level, 3 * face : 3 * face + 3, :] = swept[rows - 3 : rows, 0:width]
                base = level * slots + 3 * (face // 2)
                if face % 2 == 0:
                    edge = jnp.where(lane < 3, swept[:, 0:128], 0.0)
                    even_columns[step] = even_columns[step] + moved(edge, 0, base)
                else:
                    edge = jnp.where(lane >= 125, swept[:, width - 128 : width], 0.0)
                    odd_columns[step] = odd_columns[step] + moved(edge, 125, base)
                if step == 0:
                    rows_down[step, level, 18 + face : 19 + face, :] = wind_ref[1, level, face, 0:1, :]
                    rows_up[step, level, 18 + face : 19 + face, :] = wind_ref[
                        1, level, face, rows - 1 : rows, :
                    ]
                    base = level * slots + 9 + face // 2
                    some = lane[0:rows]
                    if face % 2 == 0:
                        edge = jnp.where(some < 1, wind_ref[0, level, face, :, 0:128], 0.0)
                        even_columns[step, 0:rows] = even_columns[step, 0:rows] + moved(
                            edge, 0, base
                        )
                    else:
                        edge = jnp.where(
                            some >= 127, wind_ref[0, level, face, :, width - 128 : width], 0.0
                        )
                        odd_columns[step, 0:rows] = odd_columns[step, 0:rows] + moved(
                            edge, 127, base
                        )
            upward, downward = row_copies(step, level)
            upward.start()
            downward.start()
            return carry

        lax.fori_loop(0, levels, sweep_east, 0)

        for own, source, to_top in ((at_top, even_columns, True), (at_low, odd_columns, False)):

            @pl.when(jnp.logical_not(own))
            def _(step=step, source=source, to_top=to_top):
                column_copy(step, source, me, to_top).start()

            @pl.when(own)
            def _(step=step, source=source, to_top=to_top):
                gathered[step, me] = source[step]
                each_other(lambda band: column_copy(step, source, band, to_top).wait_recv())
                strips = [gathered[step, band, 0:rows, :] for band in range(bands)]
                columns = jnp.concatenate(strips, 0)
                result = jnp.dot(
                    jnp.transpose(columns),
                    mirror,
                    precision=HIGHEST,
                    preferred_element_type=jnp.float32,
                )
                turned[...] = result.reshape(levels, slots, width)

        def sweep_north(level, carry, step=step):
            upward, downward = row_copies(step, level)
            upward.wait_recv()
            downward.wait_recv()
            for face in range(6):
                north_face, south_face = face, face
                if face % 2 == 0:
                    pair = ((face + 2) % 6) // 2
                    beyond = from_north[step, level, 3 * face : 3 * face + 3, :]
                    beyond = jnp.where(at_top, turned[level, 3 * pair : 3 * pair + 3, :], beyond)
                    other = (face - 1) % 6
                    before = jnp.where(
                        at_low,
                        from_south[step, level, 3 * other : 3 * other + 3, :],
                        from_south[step, level, 3 * face : 3 * face + 3, :],
                    )
                else:
                    other = (face + 1) % 6
                    beyond = jnp.where(
                        at_top,
                        from_north[step, level, 3 * other : 3 * other + 3, :],
                        from_north[step, level, 3 * face : 3 * face + 3, :],
                    )
                    pair = ((face - 2) % 6) // 2
                    before = from_south[step, level, 3 * face : 3 * face + 3, :]
                    before = jnp.where(at_low, turned[level, 3 * pair : 3 * pair + 3, :], before)
                tracer[level, face, rows : rows + 3, 0:width] = beyond
                tracer[level, face, tall - 3 : tall, 0:width] = before
                if step == 0:
                    own_row = 18 + face
                    other_row = 18 + other
                    turned_wind = turned[level, 9 + pair : 10 + pair, :]
                    beyond = from_north[step, level, own_row : own_row + 1, :]
                    before = from_south[step, level, own_row : own_row + 1, :]
                    if face % 2 == 0:
                        beyond = jnp.where(at_top, turned_wind, beyond)
                        before = jnp.where(
                            at_low, from_south[step, level, other_row : other_row + 1, :], before
                        )
                    else:
                        beyond = jnp.where(
                            at_top, from_north[step, level, other_row : other_row + 1, :], beyond
                        )
                        before = jnp.where(at_low, turned_wind, before)
                    north[level, face, 0:rows, :] = wind_ref[1, level, face]
                    north[level, face, rows : rows + 1, :] = beyond
                    north[level, face, tall - 1 : tall, :] = before
                    cells = north[level, face]
                    north[level, face] = 0.5 * (pltpu.roll(cells, 1, 0) + cells)
                swept = parabola_sweep(tracer[level, face, :, 0:width], north[level, face], 0)
                if step == 0:
                    tracer[level, face, 0:rows, 0:width] = swept[0:rows]
                else:
                    out_ref[0, level, face] = swept[0:rows]
                    parts = width // 128
                    for part in range(parts):
                        start = face * rows * parts * levels + part * levels + level
                        block_ref[pl.ds(start, rows, stride=parts * levels), :] = swept[
                            0:rows, part * 128 : (part + 1) * 128
                        ]
            return carry

        lax.fori_loop(0, levels, sweep_north, 0)

    for step in range(2):
        for own, target in ((at_top, top_edge), (at_low, low_edge)):

            @pl.when(own)
            def _(step=step, target=target):
                each_other(lambda band: edge_copy(step, band, target).wait_send())

        for own, source, to_top in ((at_top, even_columns, True), (at_low, odd_columns, False)):

            @pl.when(jnp.logical_not(own))
            def _(step=step, source=source, to_top=to_top):
                column_copy(step, source, me, to_top).wait_send()

        def sent(level, carry, step=step):
            upward, downward = row_copies(step, level)
            upward.wait_send()
            downward.wait_send()
            return carry

        lax.fori_loop(0, levels, sent, 0)


def transport(concentration, emissions, courant):
    bands = lax.axis_size("space")
    _, levels, faces, rows, width = concentration.shape
    held = -(-rows // 8) * 8
    tall = -(-(rows + 6) // 8) * 8
    full = width + 128
    slots = 128 // levels
    f32 = jnp.float32
    vmem = pl.BlockSpec(memory_space=pltpu.VMEM)
    return pl.pallas_call(
        functools.partial(transport_kernel, bands),
        out_shape=(
            jax.ShapeDtypeStruct(concentration.shape, f32),
            jax.ShapeDtypeStruct((faces * rows * (width // 128) * levels, 128), f32),
        ),
        in_specs=[vmem] * 3,
        out_specs=(vmem, vmem),
        scratch_shapes=[
            pltpu.VMEM((levels, faces, tall, full), f32),
            pltpu.VMEM((levels, faces, held, full), f32),
            pltpu.VMEM((levels, faces, tall, width), f32),
            pltpu.VMEM((levels, slots, width), f32),
            pltpu.VMEM((2, bands, held, 128), f32),
            pltpu.VMEM((2, held, 128), f32),
            pltpu.VMEM((2, held, 128), f32),
            pltpu.VMEM((2, held, 128), f32),
            pltpu.VMEM((2, held, 128), f32),
            pltpu.VMEM((2, bands, held, 128), f32),
            pltpu.VMEM((levels, slots, width), f32),
            pltpu.VMEM((2, levels, 24, width), f32),
            pltpu.VMEM((2, levels, 24, width), f32),
            pltpu.VMEM((2, levels, 24, width), f32),
            pltpu.VMEM((2, levels, 24, width), f32),
            pltpu.SemaphoreType.DMA((2, bands)),
            pltpu.SemaphoreType.DMA((2, 2)),
            pltpu.SemaphoreType.DMA((2, 2)),
            pltpu.SemaphoreType.DMA((2, bands)),
            pltpu.SemaphoreType.DMA((2, 2, levels)),
            pltpu.SemaphoreType.DMA((2, 2, levels)),
        ],
        compiler_params=pltpu.CompilerParams(
            collective_id=0, has_side_effects=True, vmem_limit_bytes=52 * 1024 * 1024
        ),
    )(concentration, emissions, courant)


def largest_divisor(number, limit):
    return max(d for d in range(1, limit + 1) if number % d == 0)


def regrid_kernel(rows, chunk, group, source_ref, target_ref, block_ref, weight_ref, sum_ref):
    step = pl.program_id(0)

    @pl.when(step == 0)
    def _():
        sum_ref[...] = jnp.zeros_like(sum_ref)

    def body(index, carry):
        products = []
        for member in range(group):
            local_tile = index * group + member
            source = source_ref[step * chunk + local_tile]
            cells = block_ref[pl.ds(pl.multiple_of(source * rows, rows), rows), :]
            products.append(
                jnp.dot(
                    cells.astype(jnp.bfloat16),
                    weight_ref[local_tile],
                    preferred_element_type=jnp.float32,
                )
            )
        for member in range(group):
            target = target_ref[step * chunk + index * group + member]
            place = pl.ds(pl.multiple_of(target * rows, rows), rows)
            sum_ref[place, :] = sum_ref[place, :] + products[member]
        return carry

    lax.fori_loop(0, chunk // group, body, 0)


def regrid(tile_source, tile_target, blocks, intersection, rows, targets):
    tiles, cells = intersection.shape[0], intersection.shape[1]
    chunk = largest_divisor(tiles, 60)
    group = largest_divisor(chunk, 20)
    summed = pl.pallas_call(
        functools.partial(regrid_kernel, rows, chunk, group),
        grid=(tiles // chunk,),
        out_shape=jax.ShapeDtypeStruct((targets * rows, cells), jnp.float32),
        in_specs=[
            pl.BlockSpec(memory_space=pltpu.SMEM),
            pl.BlockSpec(memory_space=pltpu.SMEM),
            pl.BlockSpec(memory_space=pltpu.VMEM),
            pl.BlockSpec((chunk, cells, cells), lambda step: (step, 0, 0)),
        ],
        out_specs=pl.BlockSpec(memory_space=pltpu.VMEM),
        compiler_params=pltpu.CompilerParams(vmem_limit_bytes=40 * 1024 * 1024),
        cost_estimate=pl.CostEstimate(
            flops=2 * tiles * rows * cells * cells,
            bytes_accessed=2 * tiles * cells * cells,
            transcendentals=0,
        ),
    )(tile_source, tile_target, blocks, intersection)
    return summed.reshape(targets, rows, cells)


def combine_kernel(
    scenarios,
    part_ref,
    regrid_ref,
    moment_ref,
    core_in,
    pair_sum,
    side_in,
    side_sum,
    far_in,
    mine,
    ensemble,
    core_send,
    core_recv,
    side_send,
    side_recv,
    far_send,
    far_recv,
    scen_send,
    scen_recv,
):
    me = lax.axis_index("space")
    scen = lax.axis_index("scen")
    layers = part_ref.shape[0]
    levels, blocks = regrid_ref.shape[0], regrid_ref.shape[1]
    core, side, layer = lax.rem(me, 2), lax.rem(me // 2, 2), me // 4
    sibling = {"space": me + 1 - 2 * core}
    beside = {"space": me + 2 - 4 * side}

    def far_device(other):
        return {"space": other * 4 + side * 2 + core}

    def ahead(step):
        return lax.rem(layer + step, layers)

    def other_scen(step):
        return lax.rem(scen + step, scenarios)

    barrier = pltpu.get_barrier_semaphore()
    peers = [sibling, beside]
    peers += [far_device(ahead(step)) for step in range(1, layers)]
    peers += [{"scen": other_scen(step)} for step in range(1, scenarios)]
    for peer in peers:
        pl.semaphore_signal(barrier, inc=1, device_id=peer, device_id_type=MESH)
    pl.semaphore_wait(barrier, len(peers))

    def remote(source, target, send_sem, recv_sem, device):
        return pltpu.make_async_remote_copy(
            src_ref=source,
            dst_ref=target,
            send_sem=send_sem,
            recv_sem=recv_sem,
            device_id=device,
            device_id_type=MESH,
        )

    def core_copy(at):
        return remote(
            part_ref.at[at, :, 1 - core], core_in.at[at], core_send.at[at], core_recv.at[at], sibling
        )

    def side_copy(at):
        return remote(
            pair_sum.at[at, 1 - side], side_in.at[at], side_send.at[at], side_recv.at[at], beside
        )

    def far_copy(at):
        return remote(
            side_sum.at[at], far_in.at[layer], far_send.at[at], far_recv.at[layer], far_device(at)
        )

    def far_arrival(at):
        return remote(
            side_sum.at[at], far_in.at[at], far_send.at[at], far_recv.at[at], far_device(at)
        )

    def scen_copy(to, slot):
        return remote(mine, ensemble.at[slot], scen_send.at[to], scen_recv.at[slot], {"scen": to})

    order = [ahead(step) for step in range(1, layers + 1)]
    for at in order:
        core_copy(at).start()
    for at in order:
        core_copy(at).wait_recv()
        pair_sum[at, 1 - side] = part_ref[at, 1 - side, core] + core_in[at, 1 - side]
        side_copy(at).start()
        pair_sum[at, side] = part_ref[at, side, core] + core_in[at, side]
    for at in order:
        side_copy(at).wait_recv()
        side_sum[at] = pair_sum[at, side] + side_in[at]
        if at is not order[-1]:
            far_copy(at).start()
    mine[...] = side_sum[layer]
    for at in order[:-1]:
        far_arrival(at).wait_recv()
        mine[...] = mine[...] + far_in[at]
    for step in range(1, scenarios):
        scen_copy(other_scen(step), scen).start()
    ensemble[scen] = mine[...]
    for level in range(levels):
        regrid_ref[level] = mine[pl.ds(level, blocks, stride=levels), :]
    for step in range(1, scenarios):
        scen_copy(other_scen(step), other_scen(step)).wait_recv()
    mean = ensemble[0]
    square = mean * mean
    for index in range(1, scenarios):
        member = ensemble[index]
        mean = mean + member
        square = square + member * member
    far_in[0] = mean / scenarios
    side_in[0] = square / scenarios
    for level in range(levels):
        moment_ref[0, level] = far_in[0, pl.ds(level, blocks, stride=levels), :]
        moment_ref[1, level] = side_in[0, pl.ds(level, blocks, stride=levels), :]
    for at in order:
        core_copy(at).wait_send()
        side_copy(at).wait_send()
        if at is not order[-1]:
            far_copy(at).wait_send()
    for step in range(1, scenarios):
        scen_copy(other_scen(step), scen).wait_send()


def combine(band_sums, levels):
    bands, scenarios = lax.axis_size("space"), lax.axis_size("scen")
    cells = band_sums.shape[-1]
    layers = bands // 4
    held = TGT_DEV * levels
    f32 = jnp.float32
    vmem = pl.BlockSpec(memory_space=pltpu.VMEM)
    parts = band_sums.reshape(layers, 2, 2, held, cells)
    return pl.pallas_call(
        functools.partial(combine_kernel, scenarios),
        out_shape=(
            jax.ShapeDtypeStruct((levels, TGT_DEV, cells), f32),
            jax.ShapeDtypeStruct((2, levels, TGT_DEV, cells), f32),
        ),
        in_specs=[vmem],
        out_specs=(vmem, vmem),
        scratch_shapes=[
            pltpu.VMEM((layers, 2, held, cells), f32),
            pltpu.VMEM((layers, 2, held, cells), f32),
            pltpu.VMEM((layers, held, cells), f32),
            pltpu.VMEM((layers, held, cells), f32),
            pltpu.VMEM((layers, held, cells), f32),
            pltpu.VMEM((held, cells), f32),
            pltpu.VMEM((scenarios, held, cells), f32),
        ]
        + [pltpu.SemaphoreType.DMA((layers,))] * 6
        + [pltpu.SemaphoreType.DMA((scenarios,))] * 2,
        compiler_params=pltpu.CompilerParams(
            collective_id=1, has_side_effects=True, vmem_limit_bytes=48 * 1024 * 1024
        ),
    )(parts)


def local(concentration, emissions, courant, tile_source, tile_target, intersection):
    band_count = lax.axis_size("space")
    tracer, blocks = transport(concentration, emissions, courant)
    scenarios = tracer.shape[0]
    levels = tracer.shape[1]
    batch_rows = scenarios * levels
    block_cells = intersection.shape[1]
    band_sums = regrid(
        tile_source, tile_target, blocks, intersection, batch_rows, TGT_DEV * band_count
    )
    regridded, ensemble_moments = combine(band_sums, levels)
    return (tracer, regridded[None], ensemble_moments)


def solution(mesh):
    return jax.shard_map(
        local,
        mesh=mesh,
        in_specs=(
            P("scen", None, None, "space", None),
            P("scen", None, "space", None),
            P(None, None, None, "space", None),
            P("space"),
            P("space"),
            P("space", None, None),
        ),
        out_specs=(
            P("scen", None, None, "space", None),
            P("scen", None, "space", None),
            P(None, None, "space", None),
        ),
        check_vma=False,
    )
```
